256 devices in a mesh: rep: 16 (over z, y_lo), tp: 16 (over x, y_hi, core).
Axes of the slice: x: 4, y: 4 (y_hi: 2, y_lo: 2; y = y_hi * 2 + y_lo), z: 8, core: 2. Of those that a mesh axis runs over, the one named last changes fastest.
Arguments:
- ids: int32 [128, 256], P('rep'), may hold values from 0 to 255999, as said below
- activations: bfloat16 [128, 256, 2304], P('rep', 'tp'), may hold values from -6 to 6
- cotangent: bfloat16 [128, 256, 18432], P('rep', None, 'tp'), may hold values from -6 to 6
- replica_weight: bfloat16 [16, 2304, 18432], P('rep', None, 'tp'), may hold values from -6 to 6
Outputs:
- merged: bfloat16 [2304, 18432], P('rep', 'tp')
The draws below stay inside these ranges and needn't reach their ends.
Inputs may be any that keep to these rules, and one draw needn't show every extreme that they name: Each example holds real token ids (1 or more) up to its length and the padding id 0 after it; its first token is always real and its last token is always padding.
All inputs are finite; a program needn't handle non-finite values.
Results may differ from the reference program's by a relative error of at most 0.01.
Values may be sent and summed in bfloat16 or wider, within the bound.
No kernel may reach another device: no remote copies, remote signals or barrier semaphores. Data moves between devices by JAX's collectives and lax.ppermute only.
A program may use at most 128 MiB of HBM per device.

```python
import jax
import jax.numpy as jnp
from jax import lax

D = 2304
FF = 18432
VOCAB = 256000
SEQ = 256
EX = 8
EXAMPLES = 128
N_REP = 16


def draw_ids(key, part):
    key = jax.random.fold_in(key, 7)
    key_length, key_tokens = jax.random.split(key)
    lengths = jax.random.randint(key_length, (EXAMPLES, 1), SEQ // 8, SEQ)
    tokens = jax.random.randint(key_tokens, (EXAMPLES, SEQ), 1, VOCAB)
    rows = jnp.arange(EXAMPLES)[:, None]
    positions = jnp.arange(SEQ)[None, :]
    tokens = jnp.where((rows == 0) & (positions == 0), VOCAB - 1, tokens)
    return jnp.where(positions < lengths, tokens, 0).astype(jnp.int32)


def block_scale(rng, extent, cuts, smallest, high):
    def one(position, blocks):
        draws = jax.random.uniform(jax.random.fold_in(jax.random.fold_in(rng, 6), position), (blocks,), jnp.float32, smallest / len(cuts), high / len(cuts))
        return jnp.repeat(jnp.exp(draws), extent[position] // blocks).reshape((-1,) + (1,) * (len(extent) - position - 1))

    factor_of = one(*cuts[0])
    for cut in cuts[1:]:
        factor_of = factor_of * one(*cut)
    return factor_of


def centred(rng, extent, spread, reach, pieces=(), held_as=jnp.bfloat16):
    array = spread * jax.random.normal(rng, extent, jnp.float32)
    if pieces:
        array = array * block_scale(rng, extent, pieces, -0.22, 0.18)
    return jnp.clip(array, -reach, reach).astype(held_as)


def setup_inputs(seed: int = 0) -> dict:
    key_list = jax.random.split(jax.random.key(seed), 5)
    return {
        "ids": draw_ids(jax.random.fold_in(key_list[4], 71), 0),
        "activations": centred(key_list[1], (EXAMPLES, SEQ, D), 1.0, 6.0, ((0, 16), (1, 16))),
        "cotangent": centred(key_list[2], (EXAMPLES, SEQ, FF), 1.0, 6.0, ((0, 16), (2, 16))),
        "replica_weight": centred(key_list[3], (N_REP, D, FF), 1.0, 6.0, ((0, 16), (2, 16))),
    }


def reference(ids, activations, cotangent, replica_weight):
    live = ids != 0
    masked = cotangent * live.astype(jnp.bfloat16)[:, :, None]
    inverse_counts = 1.0 / jnp.sum(live.astype(jnp.float32), axis=1)

    def accumulate(carry, replica):
        weight_total, fisher_total = carry
        fisher = jnp.zeros((D, FF), jnp.float32)
        for example in range(EX):
            row = (replica * EX + example).astype(jnp.int32)
            inputs = lax.dynamic_index_in_dim(activations, row, 0, keepdims=False)
            grads = lax.dynamic_index_in_dim(masked, row, 0, keepdims=False)
            factor = lax.dynamic_index_in_dim(inverse_counts, row, 0, keepdims=False)
            gradient = jnp.dot(inputs.T, grads, preferred_element_type=jnp.float32) * factor
            fisher = fisher + gradient * gradient
        fisher = fisher / EX
        weight = lax.dynamic_index_in_dim(replica_weight, replica.astype(jnp.int32), 0, keepdims=False)
        return (weight_total + fisher * weight.astype(jnp.float32), fisher_total + fisher), None

    zeros = jnp.zeros((D, FF), jnp.float32)
    (weight_total, fisher_total), unused = lax.scan(accumulate, (zeros, zeros), jnp.arange(N_REP, dtype=jnp.int32))
    return (weight_total / (fisher_total + 1e-6)).astype(jnp.bfloat16)
```

```python
import functools

import jax
import jax.numpy as jnp
from jax import lax
from jax.experimental import pallas as pl
from jax.experimental.pallas import tpu as pltpu
from jax.sharding import Mesh
from jax.sharding import PartitionSpec as P

ROWS = 144
PARTS = ((128, 16), (96, 32), (0, 48), (48, 48))
Y_FIRST = (False, False, False, False)
VMEM = 48 * 2**20


def blocks(part):
    if Y_FIRST[part]:
        return [(j, b) for b in range(2) for j in range(8)]
    return [(j, b) for j in range(8) for b in range(2)]


def home(z, y, j, b):
    return lax.rem(z + j, 8) * 2 + lax.rem(y + b, 2)


def order_kernel(place_ref, x_ref, *refs):
    outs, flipped, picked = refs[: len(PARTS)], refs[-2], refs[-1]
    z, y = place_ref[0], place_ref[1]
    flipped[...] = x_ref[...].T
    for part, (first, m) in enumerate(PARTS):
        for at, (j, b) in enumerate(blocks(part)):
            row = pl.multiple_of(home(z, y, j, b) * ROWS + first, 16)
            picked[at * m : (at + 1) * m, :] = flipped[pl.ds(row, m), :]
        outs[part][...] = picked[: 16 * m, :].T


def order_activations(place, x):
    tokens, d = x.shape
    return pl.pallas_call(
        order_kernel,
        out_shape=[jax.ShapeDtypeStruct((tokens, 16 * m), x.dtype) for _, m in PARTS],
        in_specs=[pl.BlockSpec(memory_space=pltpu.SMEM), pl.BlockSpec(memory_space=pltpu.VMEM)],
        out_specs=[pl.BlockSpec(memory_space=pltpu.VMEM) for _ in PARTS],
        scratch_shapes=[
            pltpu.VMEM((d, tokens), x.dtype),
            pltpu.VMEM((16 * max(m for _, m in PARTS), tokens), x.dtype),
        ],
        compiler_params=pltpu.CompilerParams(vmem_limit_bytes=VMEM),
    )(place, x)


def weight_kernel(place_ref, w_ref, *outs):
    for part, (first, m) in enumerate(PARTS):
        outs[part][0] = w_ref[0, first : first + m, :]


def order_weight(place, w):
    f = w.shape[1]

    def into(part):
        if Y_FIRST[part]:
            return lambda j, b, place: (b * 8 + j, 0, 0)
        return lambda j, b, place: (j * 2 + b, 0, 0)

    return pl.pallas_call(
        weight_kernel,
        out_shape=[jax.ShapeDtypeStruct((16, m, f), w.dtype) for _, m in PARTS],
        grid_spec=pltpu.PrefetchScalarGridSpec(
            num_scalar_prefetch=1,
            grid=(8, 2),
            in_specs=[
                pl.BlockSpec(
                    (1, ROWS, f), lambda j, b, place: (home(place[0], place[1], j, b), 0, 0)
                )
            ],
            out_specs=[
                pl.BlockSpec((1, m, f), into(part)) for part, (_, m) in enumerate(PARTS)
            ],
        ),
        compiler_params=pltpu.CompilerParams(vmem_limit_bytes=VMEM),
    )(place, w.reshape(16, ROWS, f))


def fisher_kernel(scale_ref, a_ref, g_ref, w_ref, out_ref, at_ref):
    c = a_ref.shape[2]
    for e in range(8):
        at_ref[e] = a_ref[:, 16 * e : 16 * e + 16, :].reshape(256, c).T

    def some_rows(i, carry):
        r = pl.ds(pl.multiple_of(i * 256, 256), 256)
        total = None
        for e in range(8):
            d = jnp.dot(at_ref[e, r, :], g_ref[e], preferred_element_type=jnp.float32)
            d = d * d * scale_ref[e]
            total = d if total is None else total + d
        out_ref[0, r, :] = (total * w_ref[r, :].astype(jnp.float32)).astype(jnp.bfloat16)
        out_ref[1, r, :] = total.astype(jnp.bfloat16)
        return carry

    lax.fori_loop(0, c // 256, some_rows, 0)


def fisher(scale, a, g, w):
    c, f = w.shape
    whole = pl.BlockSpec(memory_space=pltpu.VMEM)
    return pl.pallas_call(
        fisher_kernel,
        out_shape=jax.ShapeDtypeStruct((2, c, f), jnp.bfloat16),
        in_specs=[pl.BlockSpec(memory_space=pltpu.SMEM), whole, whole, whole],
        out_specs=whole,
        scratch_shapes=[pltpu.VMEM((8, c, 256), jnp.bfloat16)],
        compiler_params=pltpu.CompilerParams(vmem_limit_bytes=VMEM),
        cost_estimate=pl.CostEstimate(
            flops=2 * 2048 * c * f,
            bytes_accessed=2 * (2048 * (c + f) + 3 * c * f),
            transcendentals=0,
        ),
    )(scale, a, g, w)


def ahead(x):
    return lax.ppermute(x, "z", [(i, (i + 1) % 8) for i in range(8)])


def back(x):
    return lax.ppermute(x, "z", [(i, (i + 7) % 8) for i in range(8)])


def across(x):
    return lax.ppermute(x, "y_lo", [(0, 1), (1, 0)])


def wide(x):
    return x.astype(jnp.float32)


def narrow(x):
    return x.astype(jnp.bfloat16)


def round_z(own):
    def both(j):
        return jnp.stack([own(0, j), own(1, j)])

    up = ahead(narrow(own(0, 4)))
    down = back(narrow(own(1, 4)))
    up = ahead(narrow(jnp.stack([wide(up) + own(0, 3), own(1, 3)])))
    down = back(narrow(jnp.stack([own(0, 5), wide(down) + own(1, 5)])))
    up = ahead(narrow(wide(up) + both(2)))
    down = back(narrow(wide(down) + both(6)))
    up = ahead(narrow(wide(up) + both(1)))
    down = back(narrow(wide(down) + both(7)))
    return wide(up) + wide(down) + both(0)


def reduce_part(part, terms):
    m = PARTS[part][1]
    f = terms.shape[2]
    if Y_FIRST[part]:
        t = terms.reshape(2, 2, 8, m, f)
        other = across(t[:, 1])
        return round_z(lambda k, j: wide(t[k, 0, j]) + wide(other[k, j]))
    t = terms.reshape(2, 8, 2, m, f)
    total = round_z(lambda k, j: wide(t[k, j]))
    return total[:, 0] + wide(across(narrow(total[:, 1])))


def on_device(ids, activations, cotangent, replica_weight):
    f = cotangent.shape[2]
    place = jnp.stack([lax.axis_index("z"), lax.axis_index("y_lo")]).astype(jnp.int32)
    pieces = order_activations(place, activations.reshape(128, -1))
    gathered = [lax.all_gather(p, ("x", "y_hi", "core")) for p in pieces]
    live = ids != 0
    inverse = 1.0 / jnp.sum(live.astype(jnp.float32), axis=1)
    scale = inverse * inverse / live.shape[0]
    masked = cotangent * live.astype(jnp.bfloat16)[:, :, None]
    weights = order_weight(place, replica_weight[0])
    merged = [None] * len(PARTS)
    for part in range(len(PARTS)):
        w = weights[part].reshape(-1, f)
        terms = fisher(scale, gathered[part], masked, w)
        total = reduce_part(part, terms)
        merged[part] = narrow(total[0] / (total[1] + 1e-6))
    return jnp.concatenate([merged[part] for part in sorted(range(len(PARTS)), key=PARTS.__getitem__)])


def solution(mesh):
    fine = Mesh(
        mesh.devices.reshape(8, 2, 4, 2, 2), ("z", "y_lo", "x", "y_hi", "core")
    )
    rep, tp = ("z", "y_lo"), ("x", "y_hi", "core")
    return jax.shard_map(
        on_device,
        mesh=fine,
        in_specs=(P(rep, None), P(rep, tp, None), P(rep, None, tp), P(rep, None, tp)),
        out_specs=P(rep, tp),
        check_vma=False,
    )
```

```python
import functools

import jax
import jax.numpy as jnp
from jax import lax
from jax.experimental import pallas as pl
from jax.experimental.pallas import tpu as pltpu
from jax.sharding import Mesh
from jax.sharding import PartitionSpec as P

ROWS = 144
PARTS = ((128, 16), (96, 32), (0, 48), (48, 48))
Y_FIRST = (False, False, False, False)
VMEM = 48 * 2**20


def blocks(part):
    if Y_FIRST[part]:
        return [(j, b) for b in range(2) for j in range(8)]
    return [(j, b) for j in range(8) for b in range(2)]


def home(z, y, j, b):
    return lax.rem(z + j, 8) * 2 + lax.rem(y + b, 2)


def order_kernel(place_ref, ids_ref, x_ref, *refs):
    outs, flipped, picked = refs[: len(PARTS)], refs[-2], refs[-1]
    z, y, block = place_ref[0], place_ref[1], place_ref[2]
    tokens, d = x_ref.shape
    counts = jnp.sum((ids_ref[...] != 0).astype(jnp.float32), axis=1, keepdims=True)
    position = (lax.broadcasted_iota(jnp.int32, (16, 1), 0) + block * 16).astype(jnp.float32)
    live = jnp.concatenate([position < counts[e : e + 1] for e in range(8)])
    flipped[...] = (x_ref[...] * live.astype(jnp.float32).astype(x_ref.dtype)).T
    for part, (first, m) in enumerate(PARTS):
        for at, (j, b) in enumerate(blocks(part)):
            row = pl.multiple_of(home(z, y, j, b) * ROWS + first, 16)
            picked[at * m : (at + 1) * m, :] = flipped[pl.ds(row, m), :]
        outs[part][...] = picked[: 16 * m, :].T


def order_activations(place, ids, x):
    tokens, d = x.shape
    whole = pl.BlockSpec(memory_space=pltpu.VMEM)
    return pl.pallas_call(
        order_kernel,
        out_shape=[jax.ShapeDtypeStruct((tokens, 16 * m), x.dtype) for _, m in PARTS],
        in_specs=[pl.BlockSpec(memory_space=pltpu.SMEM), whole, whole],
        out_specs=[whole for _ in PARTS],
        scratch_shapes=[
            pltpu.VMEM((d, tokens), x.dtype),
            pltpu.VMEM((16 * max(m for _, m in PARTS), tokens), x.dtype),
        ],
        compiler_params=pltpu.CompilerParams(vmem_limit_bytes=VMEM),
        cost_estimate=pl.CostEstimate(flops=0, bytes_accessed=4 * tokens * d, transcendentals=0),
    )(place, ids, x)


def fisher_kernel(part, place_ref, scale_ref, *refs):
    pieces = [refs[2 * i : 2 * i + 2] for i in range(4)]
    g_ref, w_ref = refs[8:10]
    outs = refs[10:-3]
    a_ref, at_ref, total_ref = refs[-3:]
    first, m = PARTS[part]
    order = blocks(part)
    rows = 16 * m
    z, y, x, hi, core = [place_ref[k] for k in (0, 1, 3, 4, 5)]
    for i in range(4):
        for c in range(2):
            for h in range(2):
                block = lax.rem(x + i, 4) * 4 + lax.rem(hi + h, 2) * 2 + lax.rem(core + c, 2)
                where = pl.ds(pl.multiple_of(block * 16, 16), 16)
                for e in range(8):
                    a_ref[e, where, :] = pieces[i][c][h, 16 * e : 16 * e + 16, :]
    for e in range(8):
        at_ref[e] = a_ref[e].T
    step = total_ref.shape[0]
    for start in range(0, rows, step):
        total = None
        for e in range(8):
            d = jnp.dot(at_ref[e, start : start + step, :], g_ref[e], preferred_element_type=jnp.float32)
            d = d * d * scale_ref[e]
            total = d if total is None else total + d
        total_ref[...] = total
        for at in range(start // m, (start + step) // m):
            j, b = order[at]
            row = pl.multiple_of(home(z, y, j, b) * ROWS + first, 16)
            one = total_ref[at * m - start : (at + 1) * m - start, :]
            weighted = (one * w_ref[pl.ds(row, m), :].astype(jnp.float32)).astype(jnp.bfloat16)
            plain = one.astype(jnp.bfloat16)
            if Y_FIRST[part]:
                outs[b][0, j], outs[b][1, j] = weighted, plain
            elif j == 4:
                outs[1][b], outs[2][b] = weighted, plain
            else:
                slot = j if j < 4 else j - 1
                outs[0][0, slot, b], outs[0][1, slot, b] = weighted, plain


def fisher(part, place, scale, pieces, g, w):
    m = PARTS[part][1]
    rows = 16 * m
    f = w.shape[1]
    step = {16: 256, 32: 256, 48: 384}[m]
    whole = pl.BlockSpec(memory_space=pltpu.VMEM)
    small = pl.BlockSpec(memory_space=pltpu.SMEM)
    shapes = [(2, 8, m, f)] * 2 if Y_FIRST[part] else [(2, 7, 2, m, f), (2, m, f), (2, m, f)]
    return pl.pallas_call(
        functools.partial(fisher_kernel, part),
        out_shape=[jax.ShapeDtypeStruct(shape, jnp.bfloat16) for shape in shapes],
        in_specs=[small, small] + [whole] * 10,
        out_specs=[whole] * len(shapes),
        scratch_shapes=[
            pltpu.VMEM((8, 256, rows), jnp.bfloat16),
            pltpu.VMEM((8, rows, 256), jnp.bfloat16),
            pltpu.VMEM((step, f), jnp.float32),
        ],
        compiler_params=pltpu.CompilerParams(vmem_limit_bytes=VMEM),
        cost_estimate=pl.CostEstimate(
            flops=2 * 2048 * rows * f,
            bytes_accessed=2 * (2048 * (rows + f) + 3 * rows * f),
            transcendentals=0,
        ),
    )(place, scale, *pieces, g, w)


def ahead(x):
    return lax.ppermute(x, "z", [(i, (i + 1) % 8) for i in range(8)])


def back(x):
    return lax.ppermute(x, "z", [(i, (i + 7) % 8) for i in range(8)])


def from_x(x, hops):
    return lax.ppermute(x, "x", [((i + hops) % 4, i) for i in range(4)])


def swap(x, axis):
    return lax.ppermute(x, axis, [(0, 1), (1, 0)])


def gather_part(own):
    pair = jnp.stack([own, swap(own, "y_hi")])
    near = [pair] + [from_x(pair, hops) for hops in (1, 2, 3)]
    return [piece for p in near for piece in (p, swap(p, "core"))]


def wide(x):
    return x.astype(jnp.float32)


def narrow(x):
    return x.astype(jnp.bfloat16)


def round_z(first, own):
    def both(j):
        return jnp.stack([own(0, j), own(1, j)])

    up = ahead(first[0])
    down = back(first[1])
    up = ahead(narrow(jnp.stack([wide(up) + own(0, 3), own(1, 3)])))
    down = back(narrow(jnp.stack([own(0, 5), wide(down) + own(1, 5)])))
    up = ahead(narrow(wide(up) + both(2)))
    down = back(narrow(wide(down) + both(6)))
    up = ahead(narrow(wide(up) + both(1)))
    down = back(narrow(wide(down) + both(7)))
    return wide(up) + wide(down) + both(0)


def reduce_part(part, terms):
    if Y_FIRST[part]:
        mine, theirs = terms
        other = swap(theirs, "y_lo")

        def own(k, j):
            return wide(mine[k, j]) + wide(other[k, j])

        return round_z((narrow(own(0, 4)), narrow(own(1, 4))), own)
    rest, weighted, plain = terms
    total = round_z((weighted, plain), lambda k, j: wide(rest[k, j if j < 4 else j - 1]))
    return total[:, 0] + wide(swap(narrow(total[:, 1]), "y_lo"))


def on_device(ids, activations, cotangent, replica_weight):
    x, hi, core = lax.axis_index("x"), lax.axis_index("y_hi"), lax.axis_index("core")
    place = jnp.stack(
        [lax.axis_index("z"), lax.axis_index("y_lo"), x * 4 + hi * 2 + core, x, hi, core]
    ).astype(jnp.int32)
    ordered = order_activations(place, ids, activations.reshape(128, -1))
    inverse = 1.0 / jnp.sum((ids != 0).astype(jnp.float32), axis=1)
    scale = inverse * inverse / ids.shape[0]
    merged = [None] * len(PARTS)
    for part in range(len(PARTS)):
        pieces = gather_part(ordered[part])
        terms = fisher(part, place, scale, pieces, cotangent, replica_weight[0])
        total = reduce_part(part, terms)
        merged[part] = narrow(total[0] / (total[1] + 1e-6))
    return jnp.concatenate([merged[part] for part in sorted(range(len(PARTS)), key=PARTS.__getitem__)])


def solution(mesh):
    fine = Mesh(
        mesh.devices.reshape(8, 2, 4, 2, 2), ("z", "y_lo", "x", "y_hi", "core")
    )
    rep, tp = ("z", "y_lo"), ("x", "y_hi", "core")
    return jax.shard_map(
        on_device,
        mesh=fine,
        in_specs=(P(rep, None), P(rep, tp, None), P(rep, None, tp), P(rep, None, tp)),
        out_specs=P(rep, tp),
        check_vma=False,
    )
```

```python
import functools

import jax
import jax.numpy as jnp
from jax import lax
from jax.experimental import pallas as pl
from jax.experimental.pallas import tpu as pltpu
from jax.sharding import Mesh
from jax.sharding import PartitionSpec as P

ROWS = 144
PARTS = ((0, 64), (64, 80))
GATHERS = ((0,), (1,))
BLOCKS = [(j, b) for j in range(8) for b in range(2)]
VMEM = 48 * 2**20


def home(z, y, j, b):
    return lax.rem(z + j, 8) * 2 + lax.rem(y + b, 2)


def order_kernel(place_ref, ids_ref, x_ref, *refs):
    outs, flipped, picked = refs[: len(GATHERS)], refs[-2], refs[-1]
    z, y, block = place_ref[0], place_ref[1], place_ref[2]
    tokens, d = x_ref.shape
    counts = jnp.sum((ids_ref[...] != 0).astype(jnp.float32), axis=1, keepdims=True)
    position = (lax.broadcasted_iota(jnp.int32, (16, 1), 0) + block * 16).astype(jnp.float32)
    live = jnp.concatenate([position < counts[e : e + 1] for e in range(8)])
    flipped[...] = (x_ref[...] * live.astype(jnp.float32).astype(x_ref.dtype)).T
    for out, parts in zip(outs, GATHERS):
        at = 0
        for part in parts:
            first, m = PARTS[part]
            for j, b in BLOCKS:
                row = pl.multiple_of(home(z, y, j, b) * ROWS + first, 16)
                picked[at : at + m, :] = flipped[pl.ds(row, m), :]
                at += m
        out[...] = picked[:at, :].T


def order_activations(place, ids, x):
    tokens, d = x.shape
    whole = pl.BlockSpec(memory_space=pltpu.VMEM)
    widths = [16 * sum(PARTS[part][1] for part in parts) for parts in GATHERS]
    return pl.pallas_call(
        order_kernel,
        out_shape=[jax.ShapeDtypeStruct((tokens, c), x.dtype) for c in widths],
        in_specs=[pl.BlockSpec(memory_space=pltpu.SMEM), whole, whole],
        out_specs=[whole for _ in widths],
        scratch_shapes=[
            pltpu.VMEM((d, tokens), x.dtype),
            pltpu.VMEM((max(widths), tokens), x.dtype),
        ],
        compiler_params=pltpu.CompilerParams(vmem_limit_bytes=VMEM),
        cost_estimate=pl.CostEstimate(flops=0, bytes_accessed=4 * tokens * d, transcendentals=0),
    )(place, ids, x)


def fisher_kernel(part, column, near, place_ref, scale_ref, *refs):
    pieces, (g_hbm, w_hbm) = refs[:near], refs[near : near + 2]
    rests, firsts = refs[near + 2 : near + 4], refs[near + 4 : near + 6]
    a_ref, at_ref, g_ref, w_ref, total_ref, a_sem, g_sem, w_sem = refs[-8:]
    first, m = PARTS[part]
    rows, step = 16 * m, total_ref.shape[0]
    z, y, core = place_ref[0], place_ref[1], place_ref[3]
    load_a, load_g, load_w = [], [], []
    for e in range(8):
        for c, piece in enumerate(pieces):
            to = a_ref.at[e] if near == 1 else a_ref.at[e, :, lax.rem(core + c, 2)]
            block = piece.at[:, pl.ds(16 * e, 16), pl.ds(column, rows)]
            load_a.append(pltpu.make_async_copy(block, to, a_sem.at[e, c]))
            load_a[-1].start()
        load_g.append(pltpu.make_async_copy(g_hbm.at[e], g_ref.at[e], g_sem.at[e]))
        load_g[-1].start()
    for at, (j, b) in enumerate(BLOCKS):
        row = pl.multiple_of(home(z, y, j, b) * ROWS + first, 16)
        to = w_ref.at[pl.ds(at * m, m), :]
        load_w.append(pltpu.make_async_copy(w_hbm.at[pl.ds(row, m), :], to, w_sem.at[at]))
        load_w[-1].start()
    for start in range(0, rows, step):
        total = None
        for e in range(8):
            if start == 0:
                for load in load_a[near * e : near * e + near]:
                    load.wait()
                at_ref[e] = a_ref[e].reshape(256, rows).T
                load_g[e].wait()
            d = jnp.dot(at_ref[e, start : start + step, :], g_ref[e], preferred_element_type=jnp.float32)
            d = d * d * scale_ref[e]
            total = d if total is None else total + d
        total_ref[...] = total
        for at in range(start // m, (start + step) // m):
            load_w[at].wait()
            j, b = BLOCKS[at]
            hops = lax.rem(j + 6 * j * core, 8)
            one = total_ref[at * m - start : (at + 1) * m - start, :]
            weighted = (one * w_ref[at * m : (at + 1) * m, :].astype(jnp.float32)).astype(jnp.bfloat16)
            plain = one.astype(jnp.bfloat16)
            rests[0][hops, b], rests[1][hops, b] = weighted, plain
            if j in (1, 7):

                @pl.when(hops == 7)
                def _():
                    firsts[0][b], firsts[1][b] = weighted, plain


def fisher(part, column, place, scale, pieces, g, w):
    m = PARTS[part][1]
    rows = 16 * m
    f = w.shape[1]
    step = {16: 256, 32: 256, 48: 384, 64: 256, 80: 320}[m]
    whole = pl.BlockSpec(memory_space=pltpu.VMEM)
    small = pl.BlockSpec(memory_space=pltpu.SMEM)
    far = pl.BlockSpec(memory_space=pl.ANY)
    rest = jax.ShapeDtypeStruct((8, 2, m, f), jnp.bfloat16)
    first = jax.ShapeDtypeStruct((2, m, f), jnp.bfloat16)
    split = (16, 16, rows) if len(pieces) == 1 else (8, 2, 16, rows)
    return pl.pallas_call(
        functools.partial(fisher_kernel, part, column, len(pieces)),
        out_shape=[rest, rest, first, first],
        in_specs=[small, small] + [far] * (len(pieces) + 2),
        out_specs=[whole] * 4,
        scratch_shapes=[
            pltpu.VMEM((8,) + split, jnp.bfloat16),
            pltpu.VMEM((8, rows, 256), jnp.bfloat16),
            pltpu.VMEM(g.shape, g.dtype),
            pltpu.VMEM((rows, f), w.dtype),
            pltpu.VMEM((step, f), jnp.float32),
            pltpu.SemaphoreType.DMA((8, len(pieces))),
            pltpu.SemaphoreType.DMA((8,)),
            pltpu.SemaphoreType.DMA((16,)),
        ],
        compiler_params=pltpu.CompilerParams(vmem_limit_bytes=VMEM),
        cost_estimate=pl.CostEstimate(
            flops=2 * 2048 * rows * f,
            bytes_accessed=2 * (2048 * (rows + f) + 3 * rows * f),
            transcendentals=0,
        ),
    )(place, scale, *pieces, g, w)


def next_chip(x):
    pairs = []
    for z in range(8):
        pairs += [(2 * z, 2 * ((z + 1) % 8)), (2 * z + 1, 2 * ((z + 7) % 8) + 1)]
    return lax.ppermute(x, ("z", "core"), pairs)


def swap(x, axis):
    return lax.ppermute(x, axis, [(0, 1), (1, 0)])


def wide(x):
    return x.astype(jnp.float32)


def narrow(x):
    return x.astype(jnp.bfloat16)


def nothing(*refs):
    pass


def tie(x, *after):
    anywhere = pl.BlockSpec(memory_space=pl.ANY)
    return pl.pallas_call(
        nothing,
        out_shape=jax.ShapeDtypeStruct(x.shape, x.dtype),
        in_specs=[anywhere] * (1 + len(after)),
        out_specs=anywhere,
        input_output_aliases={0: 0},
        cost_estimate=pl.CostEstimate(flops=0, bytes_accessed=0, transcendentals=0),
    )(x, *after)


class Round:
    def __init__(self, rest, first):
        self.rest, self.left = rest, 6
        self.partial = next_chip(first)

    def hop(self, *after):
        if after:
            self.partial = tie(self.partial, *after)
        self.partial = next_chip(narrow(wide(self.partial) + wide(self.rest[self.left])))
        self.left -= 1

    def end(self):
        total = wide(self.partial) + wide(self.rest[0])
        return total[0] + wide(swap(narrow(total[1]), "y_lo"))


def on_device(ids, activations, cotangent, replica_weight):
    x, hi, core = lax.axis_index("x"), lax.axis_index("y_hi"), lax.axis_index("core")
    place = jnp.stack(
        [lax.axis_index("z"), lax.axis_index("y_lo"), x * 4 + hi * 2 + core, core]
    ).astype(jnp.int32)
    early, late = order_activations(place, ids, activations.reshape(128, -1))
    late = lax.all_gather(late, ("x", "y_hi", "core"))
    inverse = 1.0 / jnp.sum((ids != 0).astype(jnp.float32), axis=1)
    scale = inverse * inverse / ids.shape[0]
    early = jnp.broadcast_to(early[None], (8,) + early.shape)
    early = lax.all_to_all(early, ("x", "y_hi"), 0, 0, tiled=True)
    gathered = (early, swap(early, "core")), (late,)
    terms = [
        fisher(part, 0, place, scale, gathered[part], cotangent, replica_weight[0])
        for part in range(len(PARTS))
    ]
    merged = []
    for part, (*rests, first_w, first_f) in enumerate(terms):
        ways = [Round(rests[0], first_w), Round(rests[1], first_f)]
        for hop in range(1, 7):
            for way in ways:
                way.hop(*([terms[1][2]] if (part, hop) == (0, 3) else []))
        weighted, plain = [way.end() for way in ways]
        merged.append(narrow(weighted / (plain + 1e-6)))
    return jnp.concatenate(merged)


def solution(mesh):
    fine = Mesh(
        mesh.devices.reshape(8, 2, 4, 2, 2), ("z", "y_lo", "x", "y_hi", "core")
    )
    rep, tp = ("z", "y_lo"), ("x", "y_hi", "core")
    return jax.shard_map(
        on_device,
        mesh=fine,
        in_specs=(P(rep, None), P(rep, tp, None), P(rep, None, tp), P(rep, None, tp)),
        out_specs=P(rep, tp),
        check_vma=False,
    )
```

```python
import functools

import jax
import jax.numpy as jnp
from jax import lax
from jax.experimental import pallas as pl
from jax.experimental.pallas import tpu as pltpu
from jax.sharding import Mesh
from jax.sharding import PartitionSpec as P

ROWS = 144
PARTS = ((0, 48), (48, 96))
GATHERS = ((0,), (1,))
BLOCKS = [(j, b) for j in range(8) for b in range(2)]
VMEM = 18 * 2**20


def home(z, y, j, b):
    return lax.rem(z + j, 8) * 2 + lax.rem(y + b, 2)


def order_kernel(place_ref, ids_ref, x_ref, *refs):
    outs, flipped, picked = refs[: len(GATHERS)], refs[-2], refs[-1]
    z, y, block = place_ref[0], place_ref[1], place_ref[2]
    tokens, d = x_ref.shape
    counts = jnp.sum((ids_ref[...] != 0).astype(jnp.float32), axis=1, keepdims=True)
    position = (lax.broadcasted_iota(jnp.int32, (16, 1), 0) + block * 16).astype(jnp.float32)
    live = jnp.concatenate([position < counts[e : e + 1] for e in range(8)])
    flipped[...] = (x_ref[...] * live.astype(jnp.float32).astype(x_ref.dtype)).T
    for out, parts in zip(outs, GATHERS):
        at = 0
        for part in parts:
            first, m = PARTS[part]
            for j, b in BLOCKS:
                row = pl.multiple_of(home(z, y, j, b) * ROWS + first, 16)
                picked[at : at + m, :] = flipped[pl.ds(row, m), :]
                at += m
        out[...] = picked[:at, :].T


def order_activations(place, ids, x):
    tokens, d = x.shape
    whole = pl.BlockSpec(memory_space=pltpu.VMEM)
    widths = [16 * sum(PARTS[part][1] for part in parts) for parts in GATHERS]
    return pl.pallas_call(
        order_kernel,
        out_shape=[jax.ShapeDtypeStruct((tokens, c), x.dtype) for c in widths],
        in_specs=[pl.BlockSpec(memory_space=pltpu.SMEM), whole, whole],
        out_specs=[whole for _ in widths],
        scratch_shapes=[
            pltpu.VMEM((d, tokens), x.dtype),
            pltpu.VMEM((max(widths), tokens), x.dtype),
        ],
        compiler_params=pltpu.CompilerParams(vmem_limit_bytes=VMEM),
        cost_estimate=pl.CostEstimate(flops=0, bytes_accessed=4 * tokens * d, transcendentals=0),
    )(place, ids, x)


def stage_kernel(g_hbm, w_hbm, g_ref, w_ref, sem):
    loads = [pltpu.make_async_copy(g_hbm, g_ref, sem.at[0]), pltpu.make_async_copy(w_hbm, w_ref, sem.at[1])]
    for load in loads:
        load.start()
    for load in loads:
        load.wait()


def stage(g, w):
    whole = pl.BlockSpec(memory_space=pltpu.VMEM)
    return pl.pallas_call(
        stage_kernel,
        out_shape=[jax.ShapeDtypeStruct(x.shape, x.dtype) for x in (g, w)],
        in_specs=[pl.BlockSpec(memory_space=pl.ANY)] * 2,
        out_specs=[whole] * 2,
        scratch_shapes=[pltpu.SemaphoreType.DMA((2,))],
        compiler_params=pltpu.CompilerParams(vmem_limit_bytes=VMEM),
        cost_estimate=pl.CostEstimate(flops=0, bytes_accessed=4 * (g.size + w.size), transcendentals=0),
    )(g, w)


def fisher_kernel(part, column, near, place_ref, scale_ref, *refs):
    pieces, (g_ref, w_ref) = refs[:near], refs[near : near + 2]
    rests, firsts = refs[near + 2 : near + 4], refs[near + 4 : near + 6]
    a_ref, at_ref, total_ref, a_sem = refs[-4:]
    first, m = PARTS[part]
    rows, step = 16 * m, total_ref.shape[0]
    z, y, core = place_ref[0], place_ref[1], place_ref[3]
    load_a = []
    for e in range(8):
        for c, piece in enumerate(pieces):
            to = a_ref.at[e] if near == 1 else a_ref.at[e, :, lax.rem(core + c, 2)]
            block = piece.at[:, pl.ds(16 * e, 16), pl.ds(column, rows)]
            load_a.append(pltpu.make_async_copy(block, to, a_sem.at[e, c]))
            load_a[-1].start()
    for start in range(0, rows, step):
        total = None
        for e in range(8):
            if start == 0:
                for load in load_a[near * e : near * e + near]:
                    load.wait()
                at_ref[e] = a_ref[e].reshape(256, rows).T
            d = jnp.dot(at_ref[e, start : start + step, :], g_ref[e], preferred_element_type=jnp.float32)
            d = d * d * scale_ref[e]
            total = d if total is None else total + d
        total_ref[...] = total
        for at in range(start // m, (start + step) // m):
            j, b = BLOCKS[at]
            hops = lax.rem(j + 6 * j * core, 8)
            row = pl.multiple_of(home(z, y, j, b) * ROWS + first, 16)
            one = total_ref[at * m - start : (at + 1) * m - start, :]
            weighted = (one * w_ref[pl.ds(row, m), :].astype(jnp.float32)).astype(jnp.bfloat16)
            plain = one.astype(jnp.bfloat16)
            rests[0][hops, b], rests[1][hops, b] = weighted, plain
            if j in (1, 7):

                @pl.when(hops == 7)
                def _():
                    firsts[0][b], firsts[1][b] = weighted, plain


def fisher(part, column, place, scale, pieces, g, w):
    m = PARTS[part][1]
    rows = 16 * m
    f = w.shape[1]
    step = {16: 256, 32: 256, 48: 384, 64: 256, 80: 320, 96: 384}[m]
    whole = pl.BlockSpec(memory_space=pltpu.VMEM)
    small = pl.BlockSpec(memory_space=pltpu.SMEM)
    far = pl.BlockSpec(memory_space=pl.ANY)
    rest = jax.ShapeDtypeStruct((8, 2, m, f), jnp.bfloat16)
    first = jax.ShapeDtypeStruct((2, m, f), jnp.bfloat16)
    split = (16, 16, rows) if len(pieces) == 1 else (8, 2, 16, rows)
    return pl.pallas_call(
        functools.partial(fisher_kernel, part, column, len(pieces)),
        out_shape=[rest, rest, first, first],
        in_specs=[small, small] + [far] * len(pieces) + [whole] * 2,
        out_specs=[whole] * 4,
        scratch_shapes=[
            pltpu.VMEM((8,) + split, jnp.bfloat16),
            pltpu.VMEM((8, rows, 256), jnp.bfloat16),
            pltpu.VMEM((step, f), jnp.float32),
            pltpu.SemaphoreType.DMA((8, len(pieces))),
        ],
        compiler_params=pltpu.CompilerParams(vmem_limit_bytes=VMEM),
        cost_estimate=pl.CostEstimate(
            flops=2 * 2048 * rows * f,
            bytes_accessed=2 * (2048 * (rows + f) + 3 * rows * f),
            transcendentals=0,
        ),
    )(place, scale, *pieces, g, w)


def next_chip(x):
    pairs = []
    for z in range(8):
        pairs += [(2 * z, 2 * ((z + 1) % 8)), (2 * z + 1, 2 * ((z + 7) % 8) + 1)]
    return lax.ppermute(x, ("z", "core"), pairs)


def swap(x, axis):
    return lax.ppermute(x, axis, [(0, 1), (1, 0)])


def wide(x):
    return x.astype(jnp.float32)


def narrow(x):
    return x.astype(jnp.bfloat16)


def nothing(*refs):
    pass


def tie(x, *after):
    anywhere = pl.BlockSpec(memory_space=pl.ANY)
    return pl.pallas_call(
        nothing,
        out_shape=jax.ShapeDtypeStruct(x.shape, x.dtype),
        in_specs=[anywhere] * (1 + len(after)),
        out_specs=anywhere,
        input_output_aliases={0: 0},
        cost_estimate=pl.CostEstimate(flops=0, bytes_accessed=0, transcendentals=0),
    )(x, *after)


class Round:
    def __init__(self, rest, first):
        self.rest, self.left = rest, 6
        self.partial = next_chip(first)

    def wait(self, *after):
        self.partial = tie(self.partial, *after)

    def total(self):
        return wide(self.partial) + wide(self.rest[self.left])

    def hop(self):
        self.partial = next_chip(narrow(self.total()))
        self.left -= 1

    def end(self):
        total = self.total()
        return total[0] + wide(swap(narrow(total[1]), "y_lo"))


def on_device(ids, activations, cotangent, replica_weight):
    x, hi, core = lax.axis_index("x"), lax.axis_index("y_hi"), lax.axis_index("core")
    place = jnp.stack(
        [lax.axis_index("z"), lax.axis_index("y_lo"), x * 4 + hi * 2 + core, core]
    ).astype(jnp.int32)
    early, late = order_activations(place, ids, activations.reshape(128, -1))
    late = lax.all_gather(late, ("x", "y_hi", "core"))
    inverse = 1.0 / jnp.sum((ids != 0).astype(jnp.float32), axis=1)
    scale = inverse * inverse / ids.shape[0]
    early = jnp.broadcast_to(early[None], (8,) + early.shape)
    early = lax.all_to_all(early, ("x", "y_hi"), 0, 0, tiled=True)
    gathered = (early, swap(early, "core")), (late,)
    staged = stage(cotangent, replica_weight[0])
    terms = [
        fisher(part, 0, place, scale, gathered[part], *staged)
        for part in range(len(PARTS))
    ]
    ways = []
    for *rests, first_w, first_f in terms:
        ways.append([Round(rests[0], first_w), Round(rests[1], first_f)])
    early, late = ways
    for hop in range(1, 6):
        for way in early:
            if hop == 5:
                way.wait(terms[1][2])
            way.hop()
    arrived = [way.partial for way in late]
    for way in early:
        way.wait(*arrived)
        way.hop()
    for way in late:
        way.hop()
    arrived = [way.partial for way in late]
    for way in early:
        way.wait(*arrived)
    for hop in range(2, 7):
        for way in late:
            way.hop()
    merged = []
    for weighted, plain in ways:
        merged.append(narrow(weighted.end() / (plain.end() + 1e-6)))
    return jnp.concatenate(merged)


def solution(mesh):
    fine = Mesh(
        mesh.devices.reshape(8, 2, 4, 2, 2), ("z", "y_lo", "x", "y_hi", "core")
    )
    rep, tp = ("z", "y_lo"), ("x", "y_hi", "core")
    return jax.shard_map(
        on_device,
        mesh=fine,
        in_specs=(P(rep, None), P(rep, tp, None), P(rep, None, tp), P(rep, None, tp)),
        out_specs=P(rep, tp),
        check_vma=False,
    )
```
